32 devices in a mesh: gx: 2 (over x), gy: 4 (over y, core), gz: 4 (over z).
Axes of the slice: x: 2, y: 2, z: 4, core: 2. Of those that a mesh axis runs over, the one named last changes fastest.
Arguments:
- offsets: float32 [3, 4, 16, 16, 8], P(None, 'gx', 'gy', 'gz'), may hold values from 0 to 5
- species: int32 [4, 16, 16, 8], P('gx', 'gy', 'gz'), may hold values from 0 to 4
- pair_list: int32 [2, 2, 4, 4, 1024], P(None, 'gx', 'gy', 'gz'), may hold values from 0 to 1151, as said below
- pair_count: int32 [2, 4, 4], P('gx', 'gy', 'gz'), may hold values from 512 to 1024, as said below
- w_rad: float32 [8, 256], replicated, may hold values from -2 to 2
- emb_center: float32 [5, 256], replicated, may hold values from -4 to 4
- emb_neigh: float32 [5, 256], replicated, may hold values from -4 to 4
- w_embed: bfloat16 [256, 64], replicated, may hold values from -0.375 to 0.375
- w_tensor: bfloat16 [64, 32], replicated, may hold values from -0.75 to 0.75
- w_env: bfloat16 [2, 64, 32], replicated, may hold values from -0.75 to 0.75
- w_up: bfloat16 [2, 128, 256], replicated, may hold values from -0.5 to 0.5
- w_down: bfloat16 [2, 256, 64], replicated, may hold values from -0.375 to 0.375
- mix_scalar: float32 [2, 2, 32, 32], replicated, may hold values from -0.75 to 0.75
- mix_vector: float32 [2, 3, 32, 32], replicated, may hold values from -0.625 to 0.625
- w_out: float32 [64], replicated, may hold values from -0.75 to 0.75
- w_tout: float32 [32], replicated, may hold values from -1 to 1
Outputs:
- forces: float32 [3, 4, 16, 16, 8], P(None, 'gx', 'gy', 'gz')
- atom_energy: float32 [4, 16, 16, 8], P('gx', 'gy', 'gz')
The draws below stay inside these ranges and needn't reach their ends.
Inputs may be any that keep to these rules, and one draw needn't show every extreme that they name: `pair_list`: row 0 is a local atom index below 256; row 1 is a view index below 1152 naming an atom in the centre's own cell or one of the 26 cells around it, never the centre itself. `pair_count`: some domain has all 1024 slots live in every draw.
All inputs are finite; a program needn't handle non-finite values.
Results may differ from the reference program's by a relative error of at most 0.009.
Values sent between devices are 32-bit elements; how exact they have to be, the bound alone decides.
A program may use at most 64 MiB of HBM per device.

```python
import jax
import jax.numpy as jnp
from jax import lax

SCAL = 64
TENS = 32
HID = 256
NB = 8
NSPEC = 5
RC = 5
LAYERS = 2
BX = 2
BY = 4
BZ = 4
SLOTS = 8
PAIRS = 1024
NBX = 4
NBY = 16
NBZ = 16
N_GX = 2
N_GY = 4
N_GZ = 4


def lattice_of(key):
    shape = (3, NBX, NBY, NBZ, SLOTS)
    grid = jax.random.randint(key, shape, 0, 16)
    slot_pos = lax.broadcasted_iota(jnp.int32, shape, 4)
    grid = jnp.where(slot_pos == 0, grid % 4, jnp.where(slot_pos == SLOTS - 1, 12 + grid % 4, grid))
    return grid.astype(jnp.int32)


def draw_offsets(key, part):
    lattice = lattice_of(key)
    key = jax.random.fold_in(key, 13)
    shape = (3, NBX, NBY, NBZ, SLOTS)
    jitter = jax.random.uniform(key, shape, jnp.float32, -0.4, 0.4)
    return (lattice.astype(jnp.float32) + 0.5 + jitter) * (RC / 16.0)


def draw_pair_list(key, part):
    lattice = lattice_of(key)
    key = jax.random.fold_in(key, 11)
    keys = jax.random.split(key, 5)
    shape = (N_GX, N_GY, N_GZ, PAIRS)
    flat_lattice = lattice.reshape(3, -1)
    home_x = jax.random.randint(keys[0], shape, 0, BX)
    home_y = jax.random.randint(keys[1], shape, 0, BY)
    home_z = jax.random.randint(keys[2], shape, 0, BZ)
    home_slot = jax.random.randint(keys[3], shape, 0, SLOTS)
    slot_pos = lax.broadcasted_iota(jnp.int32, shape, 3)
    top_pair = slot_pos == 0
    low_pair = slot_pos == 1
    home_x = jnp.where(top_pair, BX - 1, jnp.where(low_pair, 0, home_x))
    home_y = jnp.where(top_pair, BY - 1, jnp.where(low_pair, 0, home_y))
    home_z = jnp.where(top_pair, BZ - 1, jnp.where(low_pair, 0, home_z))
    home_slot = jnp.where(top_pair, SLOTS - 1, jnp.where(low_pair, 0, home_slot))
    glob_x = lax.broadcasted_iota(jnp.int32, shape, 0) * BX + home_x
    glob_y = lax.broadcasted_iota(jnp.int32, shape, 1) * BY + home_y
    glob_z = lax.broadcasted_iota(jnp.int32, shape, 2) * BZ + home_z

    def fetch(cell_x, cell_y, cell_z, slot):
        index = ((cell_x * NBY + cell_y) * NBZ + cell_z) * SLOTS + slot
        return jnp.take(flat_lattice, index, axis=1)
    center_lat = fetch(glob_x, glob_y, glob_z, home_slot)

    def candidate(turn):
        sub = jax.random.split(jax.random.fold_in(keys[4], turn), 4)
        steps = []
        for comp in range(3):
            pick = jax.random.randint(sub[comp], shape, 0, 6)
            toward = jnp.where(center_lat[comp] < 8, -1, 1)
            steps.append(jnp.where(pick < 3, 0, jnp.where(pick < 5, toward, -toward)).astype(jnp.int32))
        slot = jax.random.randint(sub[3], shape, 0, SLOTS)
        same = (steps[0] == 0) & (steps[1] == 0) & (steps[2] == 0) & (slot == home_slot)
        slot = jnp.where(same, (slot + 1) % SLOTS, slot).astype(jnp.int32)
        other_lat = fetch((glob_x + steps[0]) % NBX, (glob_y + steps[1]) % NBY, (glob_z + steps[2]) % NBZ, slot)
        bound = jnp.zeros(shape, jnp.int32)
        for comp in range(3):
            gap = jnp.abs(16 * steps[comp] + other_lat[comp] - center_lat[comp])
            bound = bound + jnp.square(5 * gap + 4)
        return (steps[0], steps[1], steps[2], slot, bound < 6400)
    first = candidate(0)

    def advance(turn, carry):
        found = carry[4]
        fresh = candidate(turn)
        take = fresh[4] & jnp.logical_not(found)
        picked = tuple((jnp.where(take, fresh[n], carry[n]) for n in range(4)))
        return picked + (found | fresh[4],)
    step_x, step_y, step_z, other_slot, found = lax.fori_loop(1, 16, advance, first)
    step_x = jnp.where(top_pair, 1, jnp.where(low_pair, -1, step_x))
    step_y = jnp.where(top_pair, 1, jnp.where(low_pair, -1, step_y))
    step_z = jnp.where(top_pair, 1, jnp.where(low_pair, -1, step_z))
    other_slot = jnp.where(top_pair, 0, jnp.where(low_pair, SLOTS - 1, other_slot))
    center_list = ((home_x * BY + home_y) * BZ + home_z) * SLOTS + home_slot
    neighbor_list = (((home_x + 1 + step_x) * (BY + 2) + home_y + 1 + step_y) * (BZ + 2) + home_z + 1 + step_z) * SLOTS + other_slot
    return jnp.stack([center_list, neighbor_list]).astype(jnp.int32)


def draw_pair_count(key, part):
    key = jax.random.fold_in(key, 12)
    first, second = jax.random.split(key)
    total = N_GX * N_GY * N_GZ
    counts = PAIRS // 2 + jax.random.randint(first, (total,), 0, PAIRS // 2 + 1)
    chosen = jax.random.randint(second, (), 0, total)
    counts = jnp.where(jnp.arange(total) == chosen, PAIRS, counts)
    return counts.reshape(N_GX, N_GY, N_GZ).astype(jnp.int32)


def place_ends(result, stream_key, smallest, largest):
    shape = result.shape
    index_at = [jax.random.randint(jax.random.fold_in(stream_key, axis), (), 0, shape[axis]) for axis in range(len(shape))]
    result = result.at[tuple(index_at)].set(smallest)
    longest = shape.index(max(shape))
    index_at[longest] = (index_at[longest] + 1) % shape[longest]
    return result.at[tuple(index_at)].set(largest)


def normal_values(own_key, shape, scale, limit, held_as=jnp.bfloat16):
    entries = scale * jax.random.normal(own_key, shape, jnp.float32)
    return jnp.clip(entries, min=-limit, max=limit).astype(held_as)


def setup_inputs(seed: int = 0) -> dict:
    arg_keys = jax.random.split(jax.random.key(seed), 17)
    offsets = draw_offsets(jax.random.fold_in(arg_keys[16], 71), 0)
    species = place_ends(jax.random.randint(arg_keys[1], (NBX, NBY, NBZ, SLOTS), 0, NSPEC), jax.random.fold_in(arg_keys[1], 1), 0, NSPEC - 1).astype(jnp.int32)
    pair_list = draw_pair_list(jax.random.fold_in(arg_keys[16], 71), 0)
    pair_count = draw_pair_count(jax.random.fold_in(arg_keys[16], 71), 0)
    w_rad = normal_values(arg_keys[4], (NB, HID), NB ** -0.5, 2.0, jnp.float32)
    emb_center = normal_values(arg_keys[5], (NSPEC, HID), 1.0, 4.0, jnp.float32)
    emb_neigh = normal_values(arg_keys[6], (NSPEC, HID), 1.0, 4.0, jnp.float32)
    w_embed = normal_values(arg_keys[7], (HID, SCAL), HID ** -0.5, 0.375)
    w_tensor = normal_values(arg_keys[8], (SCAL, TENS), SCAL ** -0.5, 0.75)
    w_env = normal_values(arg_keys[9], (LAYERS, SCAL, TENS), SCAL ** -0.5, 0.75)
    w_up = normal_values(arg_keys[10], (LAYERS, SCAL + 2 * TENS, HID), (SCAL + 2 * TENS) ** -0.5, 0.5)
    w_down = normal_values(arg_keys[11], (LAYERS, HID, SCAL), HID ** -0.5, 0.375)
    mix_scalar = normal_values(arg_keys[12], (LAYERS, 2, TENS, TENS), (2 * TENS) ** -0.5, 0.75, jnp.float32)
    mix_vector = normal_values(arg_keys[13], (LAYERS, 3, TENS, TENS), (3 * TENS) ** -0.5, 0.625, jnp.float32)
    w_out = normal_values(arg_keys[14], (SCAL,), SCAL ** -0.5, 0.75, jnp.float32)
    w_tout = normal_values(arg_keys[15], (TENS,), TENS ** -0.5, 1.0, jnp.float32)
    return dict(offsets=offsets, species=species, pair_list=pair_list, pair_count=pair_count, w_rad=w_rad, emb_center=emb_center, emb_neigh=emb_neigh, w_embed=w_embed, w_tensor=w_tensor, w_env=w_env, w_up=w_up, w_down=w_down, mix_scalar=mix_scalar, mix_vector=mix_vector, w_out=w_out, w_tout=w_tout)


best_precision = lax.Precision.HIGHEST
soft_square = 0.25
env_scale = 0.25

def domain_energy(ext_off, ext_spec, center_list, neighbor_list, live_count, w_rad, emb_center, emb_neigh, w_embed, w_tensor, w_env, w_up, w_down, mix_scalar, mix_vector, w_out, w_tout):
    ext_x, ext_y, ext_z, slot_count = ext_off.shape[1:]
    cells_x, cells_y, cells_z = (ext_x - 2, ext_y - 2, ext_z - 2)
    cell_width = float(RC)
    grid_shape = (ext_x, ext_y, ext_z, slot_count)
    cell_grid = jnp.stack([lax.broadcasted_iota(jnp.int32, grid_shape, 0), lax.broadcasted_iota(jnp.int32, grid_shape, 1), lax.broadcasted_iota(jnp.int32, grid_shape, 2)]).astype(jnp.float32)
    position = (cell_grid * cell_width + ext_off).reshape(3, -1)
    species_flat = ext_spec.reshape(-1)
    slot_index = center_list % slot_count
    remain = center_list // slot_count
    cell_z = remain % cells_z
    remain = remain // cells_z
    cell_y = remain % cells_y
    cell_x = remain // cells_y
    home_index = ((((cell_x + 1) * ext_y + cell_y + 1) * ext_z + cell_z + 1) * slot_count + slot_index).astype(jnp.int32)
    pos_home = jnp.take(position, home_index, axis=1)
    pos_other = jnp.take(position, neighbor_list, axis=1)
    offset_vec = pos_other - pos_home
    dist_sq = lax.optimization_barrier(jnp.sum(offset_vec * offset_vec, 0))
    distance = jnp.sqrt(dist_sq + soft_square)
    direction = offset_vec / distance
    pair_rows = center_list.shape[0]
    live_mask = (lax.iota(jnp.int32, pair_rows) < live_count).astype(jnp.float32)
    envelope = live_mask * jnp.square(jnp.maximum(1.0 - dist_sq / (cell_width * cell_width), 0.0))
    frequency = (lax.iota(jnp.int32, w_rad.shape[0]) + 1).astype(jnp.float32)
    radial = jnp.sin(distance[:, None] * frequency[None, :] * (jnp.pi / cell_width)) / distance[:, None] * envelope[:, None]
    preact = jnp.dot(radial, w_rad, precision=best_precision, preferred_element_type=jnp.float32)
    preact = preact + jnp.take(emb_center, jnp.take(species_flat, home_index), axis=0) + jnp.take(emb_neigh, jnp.take(species_flat, neighbor_list), axis=0)
    hidden = jax.nn.silu(preact).astype(jnp.bfloat16)
    features = jnp.dot(hidden, w_embed, preferred_element_type=jnp.float32)
    amplitude = jnp.dot(features.astype(jnp.bfloat16), w_tensor, preferred_element_type=jnp.float32)
    harmonics = jnp.concatenate([jnp.ones((1, pair_rows), jnp.float32), direction], 0).T
    tensors = harmonics[:, :, None] * amplitude[:, None, :]
    atom_count = cells_x * cells_y * cells_z * slot_count
    for layer in range(w_env.shape[0]):
        weight = jnp.dot(features.astype(jnp.bfloat16), w_env[layer], preferred_element_type=jnp.float32) * envelope[:, None]
        contrib = harmonics[:, :, None] * weight[:, None, :]
        environment = jax.ops.segment_sum(contrib, center_list, num_segments=atom_count) * env_scale
        beside_all = jnp.take(environment, center_list, axis=0)
        scalar_part = tensors[:, 0]
        vector_part = tensors[:, 1:]
        env_scalar = beside_all[:, 0]
        env_vector = beside_all[:, 1:]
        dot_scalar = scalar_part * env_scalar
        dot_vector = lax.optimization_barrier(jnp.sum(vector_part * env_vector, 1))
        vec_first = scalar_part[:, None, :] * env_vector
        vec_second = vector_part * env_scalar[:, None, :]
        vec_cross = jnp.cross(vector_part, env_vector, axis=1)
        joined = jnp.concatenate([features, dot_scalar, dot_vector], 1).astype(jnp.bfloat16)
        hidden_mid = jax.nn.silu(jnp.dot(joined, w_up[layer], preferred_element_type=jnp.float32)).astype(jnp.bfloat16)
        features = features + jnp.dot(hidden_mid, w_down[layer], preferred_element_type=jnp.float32)
        scalar_next = jnp.dot(dot_scalar, mix_scalar[layer, 0], precision=best_precision) + jnp.dot(dot_vector, mix_scalar[layer, 1], precision=best_precision)
        vector_next = jnp.einsum('pmt,tu->pmu', vec_first, mix_vector[layer, 0], precision=best_precision)
        vector_next = vector_next + jnp.einsum('pmt,tu->pmu', vec_second, mix_vector[layer, 1], precision=best_precision)
        vector_next = vector_next + jnp.einsum('pmt,tu->pmu', vec_cross, mix_vector[layer, 2], precision=best_precision)
        tensors = jnp.concatenate([scalar_next[:, None, :], vector_next], 1)
    pair_energy = (jnp.dot(features, w_out, precision=best_precision) + jnp.dot(tensors[:, 0], w_tout, precision=best_precision)) * envelope
    return jax.ops.segment_sum(pair_energy, center_list, num_segments=atom_count)

def reference(offsets, species, pair_list, pair_count, w_rad, emb_center, emb_neigh, w_embed, w_tensor, w_env, w_up, w_down, mix_scalar, mix_vector, w_out, w_tout):
    domains_x, domains_y, domains_z = pair_count.shape
    slot_count = offsets.shape[4]
    cells_x = offsets.shape[1] // domains_x
    cells_y = offsets.shape[2] // domains_y
    cells_z = offsets.shape[3] // domains_z
    wrap_margin = ((0, 0), (1, 1), (1, 1), (1, 1), (0, 0))
    species_wrap = jnp.pad(species, wrap_margin[1:], mode='wrap')

    def energies(positions_in):
        offsets_wrap = jnp.pad(positions_in, wrap_margin, mode='wrap')

        def one_domain(domain_index):
            dom_x = domain_index // (domains_y * domains_z)
            dom_y = domain_index // domains_z % domains_y
            dom_z = domain_index % domains_z
            zero_index = jnp.zeros((), jnp.int32)
            ext_off = lax.dynamic_slice(offsets_wrap, (zero_index, dom_x * cells_x, dom_y * cells_y, dom_z * cells_z, zero_index), (3, cells_x + 2, cells_y + 2, cells_z + 2, slot_count))
            ext_spec = lax.dynamic_slice(species_wrap, (dom_x * cells_x, dom_y * cells_y, dom_z * cells_z, zero_index), (cells_x + 2, cells_y + 2, cells_z + 2, slot_count))
            center_list = pair_list[0, dom_x, dom_y, dom_z]
            neighbor_list = pair_list[1, dom_x, dom_y, dom_z]
            live_count = pair_count[dom_x, dom_y, dom_z]
            return domain_energy(ext_off, ext_spec, center_list, neighbor_list, live_count, w_rad, emb_center, emb_neigh, w_embed, w_tensor, w_env, w_up, w_down, mix_scalar, mix_vector, w_out, w_tout)
        return lax.map(jax.checkpoint(one_domain), jnp.arange(domains_x * domains_y * domains_z, dtype=jnp.int32))
    atom_values, pullback = jax.vjp(energies, offsets)
    gradient, = pullback(jnp.ones_like(atom_values))
    forces = -gradient
    atom_energy = atom_values.reshape(domains_x, domains_y, domains_z, cells_x, cells_y, cells_z, slot_count)
    atom_energy = atom_energy.transpose(0, 3, 1, 4, 2, 5, 6).reshape(domains_x * cells_x, domains_y * cells_y, domains_z * cells_z, slot_count)
    return (forces, atom_energy)
```

```python
import functools

import jax
import jax.numpy as jnp
from jax import lax
from jax.experimental import pallas as pl
from jax.experimental.pallas import tpu as pltpu
from jax.sharding import PartitionSpec as P

RC = 5.0
SOFT = 0.25
ENV_SCALE = 0.25
F32 = jnp.float32
BF = jnp.bfloat16


def dot_nn(a, b):
    return lax.dot_general(a, b, (((1,), (0,)), ((), ())), preferred_element_type=F32)


def dot_tn(a, b):
    return lax.dot_general(a, b, (((0,), (0,)), ((), ())), preferred_element_type=F32)


def dot_nt(a, b):
    return lax.dot_general(a, b, (((1,), (1,)), ((), ())), preferred_element_type=F32)


def dot_back(w, g):
    fill = 128 - w.shape[1]
    wide = jnp.concatenate([w.astype(F32), jnp.zeros((w.shape[0], fill), F32)], 1).astype(BF)
    return dot_nn(wide, jnp.concatenate([g.astype(BF), jnp.zeros((fill, g.shape[1]), BF)], 0))


def rows_sum(a):
    return jnp.sum(a, axis=0, keepdims=True)


def split2(a):
    hi = a.astype(BF)
    return hi, (a - hi.astype(F32)).astype(BF)


def column(row):
    n = row.shape[1]
    return jnp.broadcast_to(row, (128, n)).T[:, :1]


def silu_and_slope(x):
    s = 1.0 / (1.0 + jnp.exp(-x))
    h = x * s
    return h, s + h * (1.0 - s)


def floor_div(x, by):
    return jnp.floor((x + 0.5) * (1.0 / by))


def domain(dims, table, pairs, count, w_rad, emb_c, emb_n, w_embed, w_tensor, w_env, w_up, w_down,
           mix_s, mix_v, w_out, w_tout, keep=lambda n, a: a):
    bx, by, bz, slots = dims
    atoms = bx * by * bz * slots
    n = pairs.shape[1]
    centre = pairs[0:1]
    view = pairs[1:2].astype(F32)
    cell = floor_div(view, slots)
    slot = view - cell * slots
    row = floor_div(cell, bz + 2)
    vz = cell - row * (bz + 2)
    vx = floor_div(row, by + 2)
    vy = row - vx * (by + 2)

    def side(v, b):
        code = jnp.where(v < 0.5, 0.0, jnp.where(v > b + 0.5, 2.0, 1.0))
        return code, v - 1.0 - (code - 1.0) * b

    sx, lx = side(vx, bx)
    sy, ly = side(vy, by)
    sz, lz = side(vz, bz)
    block = (sx * 3 + sy) * 3 + sz
    place = (((lx * by + ly) * bz + lz) * slots + slot).astype(jnp.int32)
    cf = centre.astype(F32)
    ccell = floor_div(cf, slots)
    crow = floor_div(ccell, bz)
    cz = ccell - crow * bz
    cx = floor_div(crow, by)
    cy = crow - cx * by

    atom = lax.broadcasted_iota(jnp.int32, (atoms, n), 0)
    one_c = jnp.where(atom == centre, 1.0, 0.0).astype(BF)
    one_n = jnp.where(atom == place, 1.0, 0.0).astype(BF)

    hi, lo = split2(table)
    got = dot_nn(hi, one_n) + dot_nn(lo, one_n)
    other = jnp.where(block == 0.0, got[0:8], 0.0)
    for d in range(1, 27):
        other = other + jnp.where(block == d, got[8 * d : 8 * d + 8], 0.0)
    home = dot_nn(hi[13 * 8 : 14 * 8], one_c) + dot_nn(lo[13 * 8 : 14 * 8], one_c)
    diff = other - home
    rx = diff[0:1] + RC * (vx - 1.0 - cx)
    ry = diff[1:2] + RC * (vy - 1.0 - cy)
    rz = diff[2:3] + RC * (vz - 1.0 - cz)
    q = rx * rx + ry * ry + rz * rz
    dist = jnp.sqrt(q + SOFT)
    inv = 1.0 / dist
    y = [None, rx * inv, ry * inv, rz * inv]
    live = jnp.where(lax.broadcasted_iota(jnp.int32, (1, n), 1) < count, 1.0, 0.0)
    ramp = jnp.maximum(1.0 - q * (1.0 / (RC * RC)), 0.0)
    env = live * ramp * ramp
    freq = (lax.broadcasted_iota(jnp.int32, (8, n), 0) + 1).astype(F32) * (jnp.pi / RC)
    angle = freq * dist
    sin_d = jnp.sin(angle) * inv
    cos_d = jnp.cos(angle) * inv
    radial = sin_d * env
    kind = lax.broadcasted_iota(jnp.int32, (8, n), 0).astype(F32)
    sp_c = jnp.where(jnp.abs(kind - home[3:4]) < 0.5, 1.0, 0.0)
    sp_n = jnp.where(jnp.abs(kind - other[3:4]) < 0.5, 1.0, 0.0)
    r_hi = radial.astype(BF).astype(F32)
    r_lo = radial - r_hi
    x_pre = jnp.concatenate([r_hi, r_lo, r_hi, sp_c, sp_c, sp_n, sp_n, jnp.zeros_like(r_hi)], 0).astype(BF)

    def pair_of(a):
        h = a.astype(BF).astype(F32)
        return h, a - h

    wr_hi, wr_lo = pair_of(w_rad)
    ec_hi, ec_lo = pair_of(emb_c)
    en_hi, en_lo = pair_of(emb_n)
    w_pre = jnp.concatenate(
        [wr_hi, wr_hi, wr_lo, ec_hi, ec_lo, en_hi, en_lo, jnp.zeros_like(wr_hi)], 0
    ).astype(BF)
    hidden, slope0 = silu_and_slope(dot_tn(w_pre, x_pre))
    feat = dot_tn(w_embed, hidden.astype(BF))
    amp = dot_tn(w_tensor, feat.astype(BF))
    tens = [amp, amp * y[1], amp * y[2], amp * y[3]]

    layers = len(w_env)
    saved = []
    for k in range(layers):
        weight0 = dot_tn(w_env[k], feat.astype(BF))
        weight = weight0 * (env * ENV_SCALE)
        contrib = jnp.concatenate([weight, weight * y[1], weight * y[2], weight * y[3]], 0).astype(BF)
        environment = dot_nt(contrib, one_c)
        e_all = dot_nn(environment.astype(BF), one_c)
        t = e_all.shape[0] // 4
        e = [e_all[m * t : (m + 1) * t] for m in range(4)]
        dot_s = tens[0] * e[0]
        dot_v = tens[1] * e[1] + tens[2] * e[2] + tens[3] * e[3]
        joined = jnp.concatenate([feat, dot_s, dot_v], 0).astype(BF)
        hid, slope = silu_and_slope(dot_tn(w_up[k], joined))
        feat = feat + dot_tn(w_down[k], hid.astype(BF))
        saved.append((weight0, weight, e, tens, slope))
        scalars = joined[feat.shape[0] :]
        nxt = [dot_tn(mix_s[k], scalars)]
        if k < layers - 1:
            for m in range(1, 4):
                a, b = m % 3 + 1, (m + 1) % 3 + 1
                trio = jnp.concatenate(
                    [tens[0] * e[m], tens[m] * e[0], tens[a] * e[b] - tens[b] * e[a]], 0
                )
                nxt.append(dot_tn(mix_v[k], trio.astype(BF)))
        tens = nxt

    c_out, c_tout = column(w_out), column(w_tout)
    raw = rows_sum(feat * c_out) + rows_sum(tens[0] * c_tout)
    energy = raw * env
    e1 = energy.astype(BF).astype(F32)
    e2 = (energy - e1).astype(BF).astype(F32)
    e3 = energy - e1 - e2
    sub = lax.broadcasted_iota(jnp.int32, (8, n), 0)
    stack = jnp.where(sub == 0, e1, jnp.where(sub == 1, e2, jnp.where(sub == 2, e3, 0.0)))
    atom_energy = rows_sum(dot_nt(stack.astype(BF), one_c))

    d_env = raw
    d_feat = c_out * env
    d_tens = [c_tout * env, None, None, None]
    d_y = [None, 0.0, 0.0, 0.0]
    for k in range(layers - 1, -1, -1):
        weight0, weight, e, tens, slope = saved[k]
        d_hid = dot_back(w_down[k], d_feat)
        d_joined = dot_nn(w_up[k], (d_hid * slope).astype(BF))
        s = d_feat.shape[0]
        t = weight.shape[0]
        d_feat = keep(2 * k, d_feat + d_joined[:s])
        d_sv = d_joined[s:] + dot_back(mix_s[k], d_tens[0])
        ds, dv = d_sv[:t], d_sv[t:]
        dt = [ds * e[0], dv * e[1], dv * e[2], dv * e[3]]
        de = [ds * tens[0], dv * tens[1], dv * tens[2], dv * tens[3]]
        if d_tens[1] is not None:
            d_cross = [None] * 4
            for m in range(1, 4):
                trio = dot_back(mix_v[k], d_tens[m])
                first, second, d_cross[m] = trio[:t], trio[t : 2 * t], trio[2 * t :]
                dt[0] = dt[0] + first * e[m]
                de[m] = de[m] + first * tens[0]
                dt[m] = dt[m] + second * e[0]
                de[0] = de[0] + second * tens[m]
            for m in range(1, 4):
                a, b = m % 3 + 1, (m + 1) % 3 + 1
                dt[m] = dt[m] + e[a] * d_cross[b] - e[b] * d_cross[a]
                de[m] = de[m] + d_cross[a] * tens[b] - d_cross[b] * tens[a]
        d_environment = dot_nt(jnp.concatenate(de, 0).astype(BF), one_c)
        d_all = dot_nn(d_environment.astype(BF), one_c)
        dc = [d_all[m * t : (m + 1) * t] for m in range(4)]
        d_weight = dc[0]
        for m in range(1, 4):
            d_weight = d_weight + dc[m] * y[m]
            d_y[m] = d_y[m] + rows_sum(weight * dc[m])
        d_env = d_env + ENV_SCALE * rows_sum(weight0 * d_weight)
        d_feat = d_feat + keep(2 * k + 1, dot_back(w_env[k], d_weight * (env * ENV_SCALE)))
        d_tens = dt

    d_amp = d_tens[0]
    for m in range(1, 4):
        d_amp = d_amp + d_tens[m] * y[m]
        d_y[m] = d_y[m] + rows_sum(amp * d_tens[m])
    d_feat = d_feat + keep(2 * layers, dot_back(w_tensor, d_amp))
    d_pre = dot_back(w_embed, d_feat) * slope0
    d_radial = dot_nn(jnp.concatenate([wr_hi, wr_lo], 0).astype(BF), d_pre.astype(BF))
    d_radial = d_radial[:8] + d_radial[8:]
    d_env = d_env + rows_sum(d_radial * sin_d)
    d_dist = rows_sum(d_radial * (freq * cos_d - sin_d * inv)) * env
    d_dist = d_dist - (d_y[1] * y[1] + d_y[2] * y[2] + d_y[3] * y[3]) * inv
    d_q = d_env * live * ramp * (-2.0 / (RC * RC)) + d_dist * (0.5 * inv)
    twice = 2.0 * d_q
    fx = d_y[1] * inv + rx * twice
    fy = d_y[2] * inv + ry * twice
    fz = d_y[3] * inv + rz * twice
    force = jnp.where(sub == 0, fx, jnp.where(sub == 1, fy, jnp.where(sub == 2, fz, 0.0)))
    f_hi, f_lo = pair_of(force)
    both = jnp.concatenate([f_hi, f_lo], 0)
    own = dot_nt(both.astype(BF), one_c)
    own = own[:8] + own[8:]
    spread = jnp.concatenate([jnp.where(block == d, both, 0.0) for d in range(27)], 0).astype(BF)
    out = dot_nt(spread, one_n)
    blocks = []
    for d in range(27):
        term = -(out[16 * d : 16 * d + 8] + out[16 * d + 8 : 16 * d + 16])
        blocks.append(term + own if d == 13 else term)
    return atom_energy, blocks


def pad8(ref):
    a = ref[...]
    return jnp.concatenate([a, jnp.zeros((8 - a.shape[0], a.shape[1]), F32)], 0)


def kernel(dims, table, pairs, count, w_rad, emb_c, emb_n, w_embed, w_tensor, w_env, w_up, w_down,
           mix_s, mix_v, w_out, w_tout, energy, terms, held):
    layers = w_env.shape[0]
    every = range(layers)

    def keep(n, a):
        held[n] = a
        return held[n]

    atom_energy, blocks = domain(
        dims, table[...], pairs[...], count[...], w_rad[...], pad8(emb_c), pad8(emb_n), w_embed[...],
        w_tensor[...], [w_env[k] for k in every], [w_up[k] for k in every], [w_down[k] for k in every],
        [mix_s[k].astype(BF) for k in every], [mix_v[k].astype(BF) for k in every], w_out[...], w_tout[...], keep)
    energy[...] = atom_energy
    for d in range(27):
        terms[8 * d : 8 * d + 8, :] = blocks[d]


def ring(array, axis, by):
    size = lax.axis_size(axis)
    return lax.ppermute(array, axis, [(i, (i + by) % size) for i in range(size)])


def local(offsets, species, pair_list, pair_count, w_rad, emb_center, emb_neigh, w_embed, w_tensor, w_env,
          w_up, w_down, mix_scalar, mix_vector, w_out, w_tout):
    dims = species.shape
    atoms = dims[0] * dims[1] * dims[2] * dims[3]
    own = jnp.concatenate(
        [offsets.reshape(3, atoms), species.reshape(1, atoms).astype(F32), jnp.zeros((4, atoms), F32)], 0
    )
    table = own[None]
    for axis in ("gz", "gy", "gx"):
        table = jnp.concatenate([ring(table, axis, 1), table, ring(table, axis, -1)], 0)
    layers, tens = mix_scalar.shape[0], mix_scalar.shape[2]
    n = pair_list.shape[-1]
    vmem = pl.BlockSpec(memory_space=pltpu.VMEM)
    energy, terms, _ = pl.pallas_call(
        functools.partial(kernel, dims),
        out_shape=(
            jax.ShapeDtypeStruct((1, atoms), F32),
            jax.ShapeDtypeStruct((27 * 8, atoms), F32),
            jax.ShapeDtypeStruct((2 * layers + 1, w_env.shape[1], n), F32),
        ),
        in_specs=[vmem] * 15,
        out_specs=(vmem, vmem, vmem),
        compiler_params=pltpu.CompilerParams(vmem_limit_bytes=56 * 1024 * 1024),
    )(
        table.reshape(27 * 8, atoms), pair_list.reshape(2, n), pair_count.reshape(1, 1), w_rad, emb_center,
        emb_neigh, w_embed, w_tensor, w_env, w_up, w_down, mix_scalar.reshape(layers, 2 * tens, tens),
        mix_vector.reshape(layers, 3 * tens, tens), w_out.reshape(1, -1), w_tout.reshape(1, -1))
    terms = terms.reshape(27, 8, atoms)[:, :3]
    for axis in ("gx", "gy", "gz"):
        third = terms.shape[0] // 3
        below, mine, above = terms[:third], terms[third : 2 * third], terms[2 * third :]
        terms = mine + ring(below, axis, -1) + ring(above, axis, 1)
    return terms.reshape((3,) + dims), energy.reshape(dims)


def solution(mesh):
    return jax.shard_map(
        local,
        mesh=mesh,
        in_specs=(
            P(None, "gx", "gy", "gz", None),
            P("gx", "gy", "gz", None),
            P(None, "gx", "gy", "gz", None),
            P("gx", "gy", "gz"),
        )
        + (P(),) * 12,
        out_specs=(P(None, "gx", "gy", "gz", None), P("gx", "gy", "gz", None)),
        check_vma=False,
    )
```
